256 devices in a mesh: chan: 128 (over x_lo, z, y, core), freq: 2 (over x_hi).
Axes of the slice: x: 4 (x_hi: 2, x_lo: 2; x = x_hi * 2 + x_lo), y: 4, z: 8, core: 2. Of those that a mesh axis runs over, the one named last changes fastest.
Arguments:
- raw_spectra: float32 [4096, 2, 16, 512], P('chan', None, None, 'freq'), may hold values from -1800 to 1800
- valid_windows: int32 [4096], replicated, may hold values from 1 to 16
Outputs:
- correlations: float32 [4, 4096, 32, 128], P(None, ('chan', 'freq'))
The draws below stay inside these ranges and needn't reach their ends.
All inputs are finite; a program needn't handle non-finite values.
Results may differ from the reference program's by a relative error of at most 0.0003.
Values sent between devices are 32-bit elements; how exact they have to be, the bound alone decides.
No kernel may reach another device: no remote copies, remote signals or barrier semaphores. Data moves between devices by JAX's collectives and lax.ppermute only.
A program may use at most 192 MiB of HBM per device.

```python
import math
import jax
import jax.numpy as jnp
from jax import lax

C_DEV = 32
WINDOWS = 16
FBAND = 512
NFFT = 8192
K0 = 164
LAGS = 128
ROUNDS = 4
CHANNELS = 4096
N_CHAN = 128


def draw_raw_spectra(key, part):
    key = jax.random.fold_in(key, 11)
    key_gain, key_noise, key_common, key_couple = jax.random.split(key, 4)
    shape = (CHANNELS, 2, WINDOWS, FBAND)
    position = jnp.arange(CHANNELS, dtype=jnp.float32)
    rising = jnp.exp(math.log(3.0) * position / CHANNELS)
    gain = rising * jnp.exp(jax.random.uniform(key_gain, (CHANNELS,), minval=0.0, maxval=math.log(10.0)))
    noise = jnp.clip(jax.random.normal(key_noise, shape), -6.0, 6.0)
    common_part = 3.0 * jnp.clip(jax.random.normal(key_common, (2, WINDOWS, FBAND)), -4.0, 4.0)
    coupling = jax.random.uniform(key_couple, (CHANNELS,), minval=0.5, maxval=1.5)
    raw = gain[:, None, None, None] * (coupling[:, None, None, None] * common_part[None] + noise)
    return raw.astype(jnp.float32)


def plant(values, key, low, high):
    index_at = [jax.random.randint(jax.random.fold_in(key, axis), (), 0, length) for axis, length in enumerate(values.shape)]
    main_axis = values.shape.index(max(values.shape))
    next_to = index_at[:main_axis] + [(index_at[main_axis] + 1) % values.shape[main_axis]] + index_at[main_axis + 1:]
    return values.at[tuple(index_at)].set(low).at[tuple(next_to)].set(high)


def setup_inputs(seed: int = 0) -> dict:
    key_list = jax.random.split(jax.random.key(seed), 3)
    raw_spectra = draw_raw_spectra(jax.random.fold_in(key_list[2], 71), 0)
    valid_windows = plant(jax.random.randint(key_list[1], (CHANNELS,), 1, WINDOWS + 1), jax.random.fold_in(key_list[1], 1), 1, WINDOWS).astype(jnp.int32)
    return dict(raw_spectra=raw_spectra, valid_windows=valid_windows)


def whiten(raw_spectra):
    common_mode = lax.optimization_barrier(jnp.mean(raw_spectra, axis=0))
    centred = raw_spectra - common_mode[None]
    energy = lax.optimization_barrier(jnp.mean(centred[:, 0] * centred[:, 0] + centred[:, 1] * centred[:, 1], axis=-1))
    return centred / jnp.sqrt(energy + 1e-06)[:, None, :, None]

def lag_tables(first_bin, bin_count):
    bin_index = first_bin + jnp.arange(bin_count, dtype=jnp.int32)
    lag_index = jnp.arange(LAGS, dtype=jnp.int32) - LAGS // 2
    phase_units = bin_index[:, None] * lag_index[None, :] % NFFT
    angles = phase_units.astype(jnp.float32) * (2.0 * math.pi / NFFT)
    return (jnp.cos(angles), jnp.sin(angles))

def correlate(own_rows, own_counts, far_rows, far_counts, cos_table, sin_table):
    highest = lax.Precision.HIGHEST
    window_index = jnp.arange(own_rows.shape[2], dtype=jnp.int32)
    own_mask = (window_index[None, :] < own_counts[:, None]).astype(jnp.float32)
    far_mask = (window_index[None, :] < far_counts[:, None]).astype(jnp.float32)
    own_masked = own_rows * own_mask[:, None, :, None]
    far_masked = far_rows * far_mask[:, None, :, None]
    real_part = jnp.einsum('awf,bwf->abf', own_masked[:, 0], far_masked[:, 0], precision=highest)
    real_part = real_part + jnp.einsum('awf,bwf->abf', own_masked[:, 1], far_masked[:, 1], precision=highest)
    imag_part = jnp.einsum('awf,bwf->abf', own_masked[:, 1], far_masked[:, 0], precision=highest)
    imag_part = imag_part - jnp.einsum('awf,bwf->abf', own_masked[:, 0], far_masked[:, 1], precision=highest)
    shared_count = jnp.minimum(own_counts[:, None], far_counts[None, :]).astype(jnp.float32)
    real_part = real_part / shared_count[:, :, None]
    imag_part = imag_part / shared_count[:, :, None]
    lagged = jnp.einsum('abf,fl->abl', real_part, cos_table, precision=highest)
    lagged = lagged - jnp.einsum('abf,fl->abl', imag_part, sin_table, precision=highest)
    return lagged / math.sqrt(FBAND)

def reference(raw_spectra, valid_windows):
    whitened = whiten(raw_spectra)
    cos_table, sin_table = lag_tables(K0, FBAND)
    blocks = whitened.reshape(N_CHAN, C_DEV, 2, WINDOWS, FBAND)
    counts = valid_windows.reshape(N_CHAN, C_DEV)
    per_round = []
    for bit_number in range(ROUNDS):

        def one_block(block_index):
            partner = jnp.bitwise_xor(block_index, 1 << bit_number)
            return correlate(blocks[block_index], counts[block_index], blocks[partner], counts[partner], cos_table, sin_table)
        result = lax.map(one_block, jnp.arange(N_CHAN, dtype=jnp.int32))
        per_round.append(result.reshape(CHANNELS, C_DEV, LAGS))
    return jnp.stack(per_round, axis=0)
```

```python
import functools
import math

import jax
import jax.numpy as jnp
from jax import lax
from jax.experimental import pallas as pl
from jax.experimental.pallas import tpu as pltpu
from jax.sharding import PartitionSpec as P

F32 = jnp.float32
BF16 = jnp.bfloat16
FBAND = 512
NFFT = 8192
K0 = 164
LAGS = 128
ROUNDS = 4
WINDOWS = 16
A_TILE = 4
LANE = 128


def parity_of(index):
    return (index ^ (index >> 1) ^ (index >> 2) ^ (index >> 3)) & 1


def owner_round(parity, freq):
    return parity + 2 * freq


def edge_route(chan_count, flip):
    route = []
    for chan in range(chan_count):
        for freq in range(2):
            far = chan ^ (1 << owner_round(parity_of(chan), freq))
            route.append((chan * 2 + freq, far * 2 + (freq ^ flip)))
    return route


def xor_permute(block, bit, chan_count):
    return lax.ppermute(block, "chan", [(i, i ^ bit) for i in range(chan_count)])


def swap_freq(block):
    return lax.ppermute(block, "freq", [(0, 1), (1, 0)])


def lag_tables(first_bin, bin_count):
    bin_index = first_bin + jnp.arange(bin_count, dtype=jnp.int32)
    lag_index = jnp.arange(LAGS, dtype=jnp.int32) - LAGS // 2
    phase_units = bin_index[:, None] * lag_index[None, :] % NFFT
    angles = phase_units.astype(F32) * (2.0 * math.pi / NFFT)
    return (jnp.cos(angles), jnp.sin(angles))


def split_table(table):
    high = lax.reduce_precision(table, 8, 7)
    return jnp.concatenate([high.astype(BF16), (table - high).astype(BF16)], axis=1)


def edge_body(
    place, own0, own1_re, own1_im, far0, far1_re, far1_im, mean0, mean1, own_n, far_n, cos_t, sin_t,
    keep_ref, other_ref, far_ref, a_rows, b_rows, g_high, g_low,
):
    half = own0.shape[3]
    chans = own0.shape[2]
    hrows = chans // 2
    b0 = pl.multiple_of(place[0], hrows)
    a_keep = place[1]

    def whiten(low, high, rows, counts, put):
        for w in range(WINDOWS):
            re0 = low[0, w, rows, :] - mean0[0, pl.ds(w, 1), :]
            im0 = low[1, w, rows, :] - mean0[1, pl.ds(w, 1), :]
            re1 = high[0][w, rows, :] - mean1[0, pl.ds(w, 1), :]
            im1 = high[1][w, rows, :] - mean1[1, pl.ds(w, 1), :]
            energy = jnp.sum(re0 * re0 + im0 * im0 + re1 * re1 + im1 * im1, axis=1, keepdims=True)
            scale = lax.rsqrt(energy * (1.0 / FBAND) + 1e-06)
            scale = jnp.where(counts > float(w), scale, 0.0)
            put(w, re0 * scale, im0 * scale, re1 * scale, im1 * scale)

    def put_own(w, re0, im0, re1, im1):
        for k, (v0, v1) in enumerate(((re0, re1), (im0, im1), (re0 + im0, re1 + im1))):
            for c, v in enumerate((v0[:, :LANE], v0[:, LANE:], v1[:, :LANE], v1[:, LANE:])):
                a_rows[c, pl.ds(k * WINDOWS + w, chans, stride=3 * WINDOWS), :] = v

    def put_far(w, re0, im0, re1, im1):
        for k, (v0, v1) in enumerate(((re0 + im0, re1 + im1), (im0 - re0, im1 - re1), (re0, re1))):
            b_rows[k, w, :, :half] = v0
            b_rows[k, w, :, half:] = v1

    whiten(own0, (own1_re, own1_im), slice(0, chans), own_n[:, 0:1], put_own)
    whiten(far0, (far1_re, far1_im), pl.ds(b0, hrows), far_n[pl.ds(b0, hrows), 0:1], put_far)

    def products(t, carry):
        a0 = t * A_TILE
        for c in range(2 * half // LANE):
            lanes = slice(c * LANE, (c + 1) * LANE)
            sums = [[None] * 3 for _ in range(A_TILE)]
            for w in range(WINDOWS):
                far = [b_rows[k, w, :, lanes] for k in range(3)]
                for j in range(A_TILE):
                    for k in range(3):
                        own = a_rows[c, pl.ds((a0 + j) * (3 * WINDOWS) + k * WINDOWS + w, 1), :]
                        term = own * far[k]
                        sums[j][k] = term if w == 0 else sums[j][k] + term
            for j in range(A_TILE):
                s_im, s_re, s_both = sums[j]
                rows = pl.ds(pl.multiple_of((a0 + j) * hrows, hrows), hrows)
                for part, value in enumerate((s_both + s_re, s_both - s_im)):
                    high = value.astype(BF16)
                    at = slice(part * 2 * half + c * LANE, part * 2 * half + (c + 1) * LANE)
                    g_high[rows, at] = high
                    g_low[rows, at] = (value - high.astype(F32)).astype(BF16)
        return carry

    lax.fori_loop(0, chans // A_TILE, products, 0)
    far_counts = far_n[pl.ds(b0, hrows), :]
    group = 8

    def lagged(t, carry):
        size = group * hrows
        rows = pl.ds(pl.multiple_of(t * size, size), size)

        def project(part, table):
            at = slice(part * 2 * half, (part + 1) * 2 * half)
            both = jnp.dot(g_high[rows, at], table[...], preferred_element_type=F32)
            low = jnp.dot(g_low[rows, at], table[:, :LAGS], preferred_element_type=F32)
            return both[:, :LAGS] + both[:, LAGS:] + low

        real = project(0, cos_t)
        imag = project(1, sin_t)
        forward = real - imag
        backward = real + imag
        for j in range(group):
            a = t * group + j
            shared = jnp.minimum(far_counts, own_n[pl.ds(a, 1), :])
            scale = (1.0 / math.sqrt(FBAND)) / shared
            at = slice(j * hrows, (j + 1) * hrows)
            far_ref[:, a, :] = backward[at] * scale
            value = forward[at] * scale
            mine = (a >= a_keep) & (a < a_keep + hrows)

            @pl.when(mine)
            def _():
                keep_ref[a - a_keep] = value

            @pl.when(jnp.logical_not(mine))
            def _():
                other_ref[a - (hrows - a_keep)] = value

        return carry

    lax.fori_loop(0, chans // group, lagged, 0)


def edge(place, own0, own1_re, own1_im, far0, far1_re, far1_im, mean0, mean1, own_n, far_n, cos_t, sin_t):
    chans = own0.shape[2]
    band = 2 * own0.shape[3]
    hrows = chans // 2
    vmem = pl.BlockSpec(memory_space=pltpu.VMEM)
    return pl.pallas_call(
        edge_body,
        out_shape=(
            jax.ShapeDtypeStruct((hrows, hrows, LAGS), F32),
            jax.ShapeDtypeStruct((hrows, hrows, LAGS), F32),
            jax.ShapeDtypeStruct((hrows, chans, LAGS), F32),
        ),
        in_specs=[pl.BlockSpec(memory_space=pltpu.SMEM)] + [vmem] * 12,
        out_specs=(vmem, vmem, vmem),
        scratch_shapes=[
            pltpu.VMEM((band // LANE, chans * 3 * WINDOWS, LANE), F32),
            pltpu.VMEM((3, WINDOWS, hrows, band), F32),
            pltpu.VMEM((chans * hrows, 2 * band), BF16),
            pltpu.VMEM((chans * hrows, 2 * band), BF16),
        ],
        compiler_params=pltpu.CompilerParams(vmem_limit_bytes=40 * 1024 * 1024),
        cost_estimate=pl.CostEstimate(flops=800_000_000, bytes_accessed=5_000_000, transcendentals=0),
        name="edge",
    )(place, own0, own1_re, own1_im, far0, far1_re, far1_im, mean0, mean1, own_n, far_n, cos_t, sin_t)


def on_device(raw_spectra, valid_windows):
    chans, _, _, half = raw_spectra.shape
    hrows = chans // 2
    size = lax.axis_size("chan")
    chan_index = lax.axis_index("chan")
    freq_index = lax.axis_index("freq")
    barrier = lax.optimization_barrier

    def to_partner(block, flip):
        return lax.ppermute(block, ("chan", "freq"), edge_route(size, flip))

    def from_partner(block):
        route = [(low, high) for high, low in edge_route(size, 0)]
        return lax.ppermute(block, ("chan", "freq"), route)

    sums = jnp.sum(raw_spectra, axis=0)
    top = size // 2
    sums = sums + xor_permute(sums, top, size)
    block = jnp.transpose(raw_spectra, (1, 2, 0, 3))
    block, sums = barrier((block, sums))
    far_mine = from_partner(block)
    early = swap_freq(block[0])
    late = swap_freq(block[1])
    for bit in (1, 8, 16, 32):
        sums = barrier(sums + xor_permute(sums, bit, size))
    early, sums = barrier((early, sums))
    far_early = from_partner(early)
    for bit in (4, 2):
        sums = barrier(sums + xor_permute(sums, bit, size))
    mean = sums / (size * chans)
    mean_other = swap_freq(mean)
    late, mean_other = barrier((late, mean_other))
    far_late = from_partner(late)

    parity = parity_of(chan_index)
    my_round = owner_round(parity, freq_index)
    partner = chan_index ^ (1 << my_round)

    def counts(index):
        part = lax.dynamic_slice_in_dim(valid_windows, index * chans, chans)
        return jnp.broadcast_to(part.astype(F32)[:, None], (chans, LANE))

    mine_t = lag_tables(K0 + freq_index * half, half)
    other_t = lag_tables(K0 + (1 - freq_index) * half, half)
    cos_t, sin_t = [split_table(jnp.concatenate(pair, axis=0)) for pair in zip(mine_t, other_t)]

    def work(b0):
        place = jnp.stack([b0, freq_index * hrows]).astype(jnp.int32)
        return edge(
            place, block, early, late, far_mine, far_early, far_late,
            mean, mean_other, counts(chan_index), counts(partner), cos_t, sin_t,
        )

    b_first = (1 - freq_index) * hrows
    b_second = freq_index * hrows
    keep1, other1, far1 = work(b_first)
    far1 = to_partner(far1, 1)
    other1 = swap_freq(other1)
    keep2, other2, far2 = work(b_second)
    far2 = to_partner(far2, 0)
    other2 = swap_freq(other2)

    out = jnp.zeros((ROUNDS, hrows, chans, LAGS), F32)

    def place_at(out, part, at_round, at_row):
        zero = jnp.int32(0)
        return lax.dynamic_update_slice(out, part[None], (at_round, zero, at_row, zero))

    other_round = owner_round(parity, 1 - freq_index)
    out = place_at(out, keep1, my_round, b_first)
    out = place_at(out, keep2, my_round, b_second)
    zero = jnp.int32(0)
    out = place_at(out, far1, owner_round(1 - parity, 1 - freq_index), zero)
    out = place_at(out, other1, other_round, b_second)
    out = place_at(out, other2, other_round, b_first)
    out = place_at(out, far2, owner_round(1 - parity, freq_index), zero)
    return out


def solution(mesh):
    return jax.shard_map(
        on_device,
        mesh=mesh,
        in_specs=(P("chan", None, None, "freq"), P()),
        out_specs=P(None, ("chan", "freq"), None, None),
        check_vma=False,
    )
```

```python
import functools
import math

import jax
import jax.numpy as jnp
import ml_dtypes
import numpy as np
from jax import lax
from jax.experimental import pallas as pl
from jax.experimental.pallas import tpu as pltpu
from jax.sharding import PartitionSpec as P

F32 = jnp.float32
BF16 = jnp.bfloat16
FBAND = 512
NFFT = 8192
K0 = 164
LAGS = 128
ROUNDS = 4
WINDOWS = 16
CHANNELS = 4096
A_TILE = 4
LANE = 128


def parity_of(index):
    return (index ^ (index >> 1) ^ (index >> 2) ^ (index >> 3)) & 1


def owner_round(parity, freq):
    return 2 * parity + freq


def edge_route(chan_count, flip):
    route = []
    for chan in range(chan_count):
        for freq in range(2):
            far = chan ^ (1 << owner_round(parity_of(chan), freq))
            route.append((chan * 2 + freq, far * 2 + (freq ^ flip)))
    return route


def from_chan(block, source, chan_count):
    return lax.ppermute(block, "chan", [(source(i), i) for i in range(chan_count)])


def step_y(chan, by):
    return (chan & ~6) | (((chan >> 1) + by) % 4 << 1)


def step_z(chan, by):
    return (chan & ~56) | (((chan >> 3) + by) % 8 << 3)


def sum_over_chan(sums, size, order, hooks):
    top = size // 2
    steps = {
        "core": [lambda i: i ^ 1],
        "z1": [lambda i: i ^ 8],
        "z": [lambda i: step_z(i, 4), lambda i: step_z(i, 2), lambda i: step_z(i, -2)],
        "y": [lambda i: step_y(i, 2), lambda i: step_y(i, 1), lambda i: step_y(i, -1)],
        "y2": [lambda i: i ^ 4],
        "y1": [lambda i: i ^ 2],
    }
    for name in order:
        sums = sum((from_chan(sums, source, size) for source in steps[name]), sums)
        sums = lax.optimization_barrier(sums)
        if name in hooks:
            sums = hooks[name](sums)
    far = swap_freq(sums)
    near = from_chan(sums, lambda i: i ^ top, size)
    diagonal = lax.ppermute(
        sums, ("chan", "freq"), [(d, d ^ (2 * top) ^ 1) for d in range(2 * size)]
    )
    return sums, near, far, diagonal


def swap_freq(block):
    return lax.ppermute(block, "freq", [(0, 1), (1, 0)])


def lag_tables():
    bins = K0 + np.arange(FBAND)
    lags = np.arange(LAGS) - LAGS // 2
    angles = (bins[:, None] * lags[None, :] % NFFT) * (2.0 * math.pi / NFFT)
    tables = []
    for table in (np.cos(angles), np.sin(angles)):
        high = table.astype(ml_dtypes.bfloat16)
        low = (table - high.astype(np.float64)).astype(ml_dtypes.bfloat16)
        tables.append(np.concatenate([high, low], axis=1))
    return tables


def channel_counts(windows, chan, chans):
    per_row = LANE // chans
    row = windows[pl.ds(chan // per_row, 1), :]
    lanes = lax.broadcasted_iota(jnp.int32, (chans, LANE), 1)
    first = lax.broadcasted_iota(jnp.int32, (chans, LANE), 0) + chan % per_row * chans
    picked = jnp.where(lanes == first, row, 0).astype(F32)
    return jnp.sum(picked, axis=1, keepdims=True)


def means(sums):
    sum0, near0, sum1, near1 = sums
    return [
        (total[part] + near[part]) * (1.0 / CHANNELS)
        for total, near in ((sum0, near0), (sum1, near1))
        for part in range(2)
    ]


def whiten(low, high, mean, count):
    re0, im0 = low[0] - mean[0], low[1] - mean[1]
    re1, im1 = high[0] - mean[2], high[1] - mean[3]
    energy = jnp.sum(re0 * re0 + im0 * im0 + re1 * re1 + im1 * im1, axis=1, keepdims=True)
    scale = lax.rsqrt(energy * (1.0 / FBAND) + 1e-06)
    window = lax.broadcasted_iota(jnp.int32, (WINDOWS, LANE), 0).astype(F32)
    scale = jnp.where(window < count, scale, 0.0)
    re, im = [], []
    for real, imag in ((re0, im0), (re1, im1)):
        for lane in range(0, real.shape[1], LANE):
            re.append(real[:, lane : lane + LANE] * scale)
            im.append(imag[:, lane : lane + LANE] * scale)
    return re, im


def own_body(
    place, raw, other, sum0, near0, sum1, near1, windows, all_tables,
    a_rows, table, own_n, far_n, buf, sem, table_sem,
):
    chans, _, _, half = raw.shape
    step = 8
    fetches = []
    for c in range(chans // step):
        at = pl.ds(c * step, step)
        for k, source in enumerate((raw, other)):
            fetches.append(pltpu.make_async_copy(source.at[at], buf.at[k, at], sem.at[k, c]))
    for fetch in fetches:
        fetch.start()
    first_bin = pl.multiple_of(place[1] * (half // (chans // 2)), half)
    table_fetch = pltpu.make_async_copy(
        all_tables.at[:, pl.ds(first_bin, 2 * half), :], table, table_sem
    )
    table_fetch.start()
    own_n[...] = jnp.broadcast_to(channel_counts(windows, place[2], chans), (chans, LANE))
    far_n[...] = jnp.broadcast_to(channel_counts(windows, place[3], chans), (chans, LANE))
    mean = means((sum0, near0, sum1, near1))
    for c in range(chans // step):
        fetches[2 * c].wait()
        fetches[2 * c + 1].wait()

        def channel(k, carry):
            a = c * step + k
            re, im = whiten(buf[0, a], buf[1, a], mean, own_n[pl.ds(a, 1), :])
            for lane, (v, u) in enumerate(zip(re, im)):
                for plane, value in enumerate((v, u, v + u)):
                    first = pl.multiple_of(a * (3 * WINDOWS) + plane * WINDOWS, WINDOWS)
                    a_rows[lane, pl.ds(first, WINDOWS), :] = value
            return carry

        lax.fori_loop(0, step, channel, 0, unroll=True)
    table_fetch.wait()


def whiten_own(place, raw, other, sums, windows, all_tables):
    chans, _, _, half = raw.shape
    vmem = pl.BlockSpec(memory_space=pltpu.VMEM)
    anywhere = pl.BlockSpec(memory_space=pl.ANY)
    counts = jax.ShapeDtypeStruct((chans, LANE), F32)
    return pl.pallas_call(
        own_body,
        out_shape=(
            jax.ShapeDtypeStruct((2 * half // LANE, chans * 3 * WINDOWS, LANE), F32),
            jax.ShapeDtypeStruct((2, 2 * half, 2 * LAGS), BF16),
            counts,
            counts,
        ),
        in_specs=[pl.BlockSpec(memory_space=pltpu.SMEM)] + [anywhere] * 2 + [vmem] * 5 + [anywhere],
        out_specs=(vmem, vmem, vmem, vmem),
        scratch_shapes=[
            pltpu.VMEM((2, *raw.shape), F32),
            pltpu.SemaphoreType.DMA((2, chans // 8)),
            pltpu.SemaphoreType.DMA,
        ],
        compiler_params=pltpu.CompilerParams(vmem_limit_bytes=12 * 1024 * 1024),
        name="own",
    )(place, raw, other, *sums, windows, all_tables)


def edge_body(first, place, a_rows, far0, far1, table, sum0, near0, sum1, near1, own_n, far_n, *refs):
    if first:
        keep_ref, other_ref, far_ref, b_rows, g_high, g_low, far_buf, sem = refs
    else:
        keep1, other1, keep_ref, other_ref, far_ref, b_rows, g_high, g_low, far_buf, sem = refs
    chans, _, _, half = far0.shape
    hrows = chans // 2
    b0 = pl.multiple_of(place[0], hrows)
    a_keep = place[1]
    b_rows_at = pl.ds(b0, hrows)
    fetches = [
        pltpu.make_async_copy(source.at[b_rows_at], far_buf.at[k], sem.at[k])
        for k, source in enumerate((far0, far1))
    ]
    for fetch in fetches:
        fetch.start()
    mean = means((sum0, near0, sum1, near1))
    for fetch in fetches:
        fetch.wait()

    def channel(b, carry):
        re, im = whiten(far_buf[0, b], far_buf[1, b], mean, far_n[pl.ds(b0 + b, 1), :])
        for lane, (v, u) in enumerate(zip(re, im)):
            for plane, value in enumerate((v + u, u - v, v)):
                at = pl.ds(plane * WINDOWS * hrows + b, WINDOWS, stride=hrows)
                b_rows[lane, at, :] = value
        return carry

    lax.fori_loop(0, hrows, channel, 0, unroll=True)

    def products(t, carry):
        a0 = t * A_TILE
        for c in range(2 * half // LANE):
            sums = [[None] * 3 for _ in range(A_TILE)]
            for w in range(WINDOWS):
                far = [
                    b_rows[c, pl.ds((k * WINDOWS + w) * hrows, hrows), :] for k in range(3)
                ]
                for j in range(A_TILE):
                    for k in range(3):
                        own = a_rows[c, pl.ds((a0 + j) * (3 * WINDOWS) + k * WINDOWS + w, 1), :]
                        term = own * far[k]
                        sums[j][k] = term if w == 0 else sums[j][k] + term
            for j in range(A_TILE):
                s_im, s_re, s_both = sums[j]
                rows = pl.ds(pl.multiple_of((a0 + j) * hrows, hrows), hrows)
                for part, value in enumerate((s_both + s_re, s_both - s_im)):
                    high = value.astype(BF16)
                    at = slice(part * 2 * half + c * LANE, part * 2 * half + (c + 1) * LANE)
                    g_high[rows, at] = high
                    g_low[rows, at] = (value - high.astype(F32)).astype(BF16)
        return carry

    lax.fori_loop(0, chans // A_TILE, products, 0)
    far_counts = far_n[pl.ds(b0, hrows), :]
    group = 8

    def lagged(t, carry):
        size = group * hrows
        rows = pl.ds(pl.multiple_of(t * size, size), size)

        def project(part):
            at = slice(2 * part * half, 2 * (part + 1) * half)
            both = jnp.dot(g_high[rows, at], table[part], preferred_element_type=F32)
            low = jnp.dot(g_low[rows, at], table[part, :, :LAGS], preferred_element_type=F32)
            return both[:, :LAGS] + both[:, LAGS:] + low

        real = project(0)
        imag = project(1)
        forward = real - imag
        backward = real + imag
        for j in range(group):
            a = t * group + j
            shared = jnp.minimum(far_counts, own_n[pl.ds(a, 1), :])
            scale = (1.0 / math.sqrt(FBAND)) / shared
            at = slice(j * hrows, (j + 1) * hrows)
            far_ref[:, a, :] = backward[at] * scale
            value = forward[at] * scale
            mine = (a >= a_keep) & (a < a_keep + hrows)

            spot = slice(None) if first else b_rows_at

            @pl.when(mine)
            def _():
                keep_ref[a - a_keep, spot, :] = value

            @pl.when(jnp.logical_not(mine))
            def _():
                other_ref[a - (hrows - a_keep), spot, :] = value

        return carry

    lax.fori_loop(0, chans // group, lagged, 0)
    if not first:
        before = pl.ds(pl.multiple_of(hrows - b0, hrows), hrows)
        keep_ref[:, before, :] = keep1[...]
        other_ref[:, before, :] = other1[...]


def edge(place, a_rows, far, table, sums, counts, before=()):
    chans, _, _, half = far[0].shape
    band = 2 * half
    hrows = chans // 2
    vmem = pl.BlockSpec(memory_space=pltpu.VMEM)
    anywhere = pl.BlockSpec(memory_space=pl.ANY)
    mine = jax.ShapeDtypeStruct((hrows, chans if before else hrows, LAGS), F32)
    return pl.pallas_call(
        functools.partial(edge_body, not before),
        out_shape=(mine, mine, jax.ShapeDtypeStruct((hrows, chans, LAGS), F32)),
        in_specs=[pl.BlockSpec(memory_space=pltpu.SMEM), vmem]
        + [anywhere] * 2 + [vmem] * (7 + len(before)),
        out_specs=(vmem, vmem, vmem),
        scratch_shapes=[
            pltpu.VMEM((band // LANE, 3 * WINDOWS * hrows, LANE), F32),
            pltpu.VMEM((chans * hrows, 2 * band), BF16),
            pltpu.VMEM((chans * hrows, 2 * band), BF16),
            pltpu.VMEM((2, hrows, 2, WINDOWS, half), F32),
            pltpu.SemaphoreType.DMA((2,)),
        ],
        compiler_params=pltpu.CompilerParams(vmem_limit_bytes=20 * 1024 * 1024),
        cost_estimate=pl.CostEstimate(flops=1_000_000, bytes_accessed=10_000, transcendentals=0),
        name="edge",
    )(place, a_rows, *far, table, *sums, *counts, *before)


def on_device(raw_spectra, valid_windows):
    chans, _, _, half = raw_spectra.shape
    hrows = chans // 2
    size = lax.axis_size("chan")
    chan_index = lax.axis_index("chan")
    freq_index = lax.axis_index("freq")
    barrier = lax.optimization_barrier

    def to_partner(block, flip):
        return lax.ppermute(block, ("chan", "freq"), edge_route(size, flip))

    def from_partner(block):
        route = [(high, low) for low, high in edge_route(size, 0)]
        return lax.ppermute(block, ("chan", "freq"), route)

    parity = parity_of(chan_index)
    my_round = owner_round(parity, freq_index)
    partner = chan_index ^ (1 << my_round)

    sums = jnp.sum(raw_spectra, axis=0)
    other = swap_freq(raw_spectra)
    far = {}

    def after_z1(sums):
        held, sums = barrier((raw_spectra, sums))
        far["mine"] = from_partner(held)
        return sums

    def after_core(sums):
        far["own"], far["mine"], sums = barrier((other, far["mine"], sums))
        far["other"] = from_partner(far["own"])
        return sums

    sums = sum_over_chan(
        sums, size, ("z1", "z", "y", "core"), {"z1": after_z1, "core": after_core}
    )
    windows = valid_windows.reshape(-1, LANE)

    def at(b0):
        return jnp.stack([b0, freq_index * hrows, chan_index, partner]).astype(jnp.int32)

    all_tables = np.stack(lag_tables())
    all_tables = jnp.asarray(np.concatenate([all_tables, all_tables[:, :half]], axis=1))
    a_rows, table, *counts = whiten_own(at(0), raw_spectra, far["own"], sums, windows, all_tables)

    def work(b0, before=()):
        return edge(at(b0), a_rows, (far["mine"], far["other"]), table, sums, counts, before)

    keep, other, far1 = work((1 - freq_index) * hrows)
    far1 = to_partner(far1, 1)
    keep, other, far2 = work(freq_index * hrows, (keep, other))
    other = swap_freq(other)
    far1, far2 = barrier((far1, far2))
    far2 = to_partner(far2, 0)

    index = lax.broadcasted_iota(jnp.int32, (ROUNDS, 1, 1, 1), 0)
    own_pair = index // 2 == parity
    same_freq = index % 2 == freq_index
    return jnp.where(
        own_pair, jnp.where(same_freq, keep, other), jnp.where(same_freq, far2, far1)
    )


def solution(mesh):
    return jax.shard_map(
        on_device,
        mesh=mesh,
        in_specs=(P("chan", None, None, "freq"), P()),
        out_specs=P(None, ("chan", "freq"), None, None),
        check_vma=False,
    )
```

```python
import functools
import math

import jax
import jax.numpy as jnp
import ml_dtypes
import numpy as np
from jax import lax
from jax.experimental import pallas as pl
from jax.experimental.pallas import tpu as pltpu
from jax.sharding import PartitionSpec as P

F32 = jnp.float32
BF16 = jnp.bfloat16
FBAND = 512
NFFT = 8192
K0 = 164
LAGS = 128
ROUNDS = 4
WINDOWS = 16
CHANNELS = 4096
A_TILE = 4
LANE = 128


def parity_of(index):
    return (index ^ (index >> 1) ^ (index >> 2) ^ (index >> 3)) & 1


def owner_round(parity, freq):
    return 2 * parity + freq


def edge_route(chan_count, flip):
    route = []
    for chan in range(chan_count):
        for freq in range(2):
            far = chan ^ (1 << owner_round(parity_of(chan), freq))
            route.append((chan * 2 + freq, far * 2 + (freq ^ flip)))
    return route


def from_chan(block, source, chan_count):
    return lax.ppermute(block, "chan", [(source(i), i) for i in range(chan_count)])


def step_y(chan, by):
    return (chan & ~6) | (((chan >> 1) + by) % 4 << 1)


def step_z(chan, by):
    return (chan & ~56) | (((chan >> 3) + by) % 8 << 3)


def sum_over_chan(sums, size, order, hooks):
    top = size // 2
    steps = {
        "core": [lambda i: i ^ 1],
        "z1": [lambda i: i ^ 8],
        "z": [lambda i: step_z(i, 4), lambda i: step_z(i, 2), lambda i: step_z(i, -2)],
        "y": [lambda i: step_y(i, 2), lambda i: step_y(i, 1), lambda i: step_y(i, -1)],
        "y2": [lambda i: i ^ 4],
        "y1": [lambda i: i ^ 2],
    }
    for name in order:
        sums = sum((from_chan(sums, source, size) for source in steps[name]), sums)
        sums = lax.optimization_barrier(sums)
        if name in hooks:
            sums = hooks[name](sums)
    far = swap_freq(sums)
    near = from_chan(sums, lambda i: i ^ top, size)
    diagonal = lax.ppermute(
        sums, ("chan", "freq"), [(d, d ^ (2 * top) ^ 1) for d in range(2 * size)]
    )
    return sums, near, far, diagonal


def swap_freq(block):
    return lax.ppermute(block, "freq", [(0, 1), (1, 0)])


def lag_tables():
    bins = K0 + np.arange(FBAND)
    lags = np.arange(LAGS) - LAGS // 2
    angles = (bins[:, None] * lags[None, :] % NFFT) * (2.0 * math.pi / NFFT)
    tables = []
    for table in (np.cos(angles), np.sin(angles)):
        high = table.astype(ml_dtypes.bfloat16)
        low = (table - high.astype(np.float64)).astype(ml_dtypes.bfloat16)
        tables.append(np.concatenate([high, low], axis=1))
    return tables


def channel_counts(windows, chan, chans):
    per_row = LANE // chans
    row = windows[pl.ds(chan // per_row, 1), :]
    lanes = lax.broadcasted_iota(jnp.int32, (chans, LANE), 1)
    first = lax.broadcasted_iota(jnp.int32, (chans, LANE), 0) + chan % per_row * chans
    picked = jnp.where(lanes == first, row, 0).astype(F32)
    return jnp.sum(picked, axis=1, keepdims=True)


def means(sums):
    sum0, near0, sum1, near1 = sums
    return [
        (total[part] + near[part]) * (1.0 / CHANNELS)
        for total, near in ((sum0, near0), (sum1, near1))
        for part in range(2)
    ]


def whiten(low, high, mean, count):
    re0, im0 = low[0] - mean[0], low[1] - mean[1]
    re1, im1 = high[0] - mean[2], high[1] - mean[3]
    energy = jnp.sum(re0 * re0 + im0 * im0 + re1 * re1 + im1 * im1, axis=1, keepdims=True)
    scale = lax.rsqrt(energy * (1.0 / FBAND) + 1e-06)
    window = lax.broadcasted_iota(jnp.int32, (WINDOWS, LANE), 0).astype(F32)
    scale = jnp.where(window < count, scale, 0.0)
    re, im = [], []
    for real, imag in ((re0, im0), (re1, im1)):
        for lane in range(0, real.shape[1], LANE):
            re.append(real[:, lane : lane + LANE] * scale)
            im.append(imag[:, lane : lane + LANE] * scale)
    return re, im


def own_body(
    place, raw, other, sum0, near0, sum1, near1, windows, all_tables,
    a_rows, table, own_n, far_n, buf, sem, table_sem,
):
    chans, _, _, half = raw.shape
    step = 8
    fetches = []
    for c in range(chans // step):
        at = pl.ds(c * step, step)
        for k, source in enumerate((raw, other)):
            fetches.append(pltpu.make_async_copy(source.at[at], buf.at[k, at], sem.at[k, c]))
    for fetch in fetches:
        fetch.start()
    first_bin = pl.multiple_of(place[1] * (half // (chans // 2)), half)
    table_fetch = pltpu.make_async_copy(
        all_tables.at[:, pl.ds(first_bin, 2 * half), :], table, table_sem
    )
    table_fetch.start()
    own_n[...] = jnp.broadcast_to(channel_counts(windows, place[2], chans), (chans, LANE))
    far_n[...] = jnp.broadcast_to(channel_counts(windows, place[3], chans), (chans, LANE))
    mean = means((sum0, near0, sum1, near1))
    for c in range(chans // step):
        fetches[2 * c].wait()
        fetches[2 * c + 1].wait()

        def channel(k, carry):
            a = c * step + k
            re, im = whiten(buf[0, a], buf[1, a], mean, own_n[pl.ds(a, 1), :])
            for lane, (v, u) in enumerate(zip(re, im)):
                for plane, value in enumerate((v, u, v + u)):
                    first = pl.multiple_of(a * (3 * WINDOWS) + plane * WINDOWS, WINDOWS)
                    a_rows[lane, pl.ds(first, WINDOWS), :] = value
            return carry

        lax.fori_loop(0, step, channel, 0, unroll=True)
    table_fetch.wait()


def whiten_own(place, raw, other, sums, windows, all_tables):
    chans, _, _, half = raw.shape
    vmem = pl.BlockSpec(memory_space=pltpu.VMEM)
    anywhere = pl.BlockSpec(memory_space=pl.ANY)
    counts = jax.ShapeDtypeStruct((chans, LANE), F32)
    return pl.pallas_call(
        own_body,
        out_shape=(
            jax.ShapeDtypeStruct((2 * half // LANE, chans * 3 * WINDOWS, LANE), F32),
            jax.ShapeDtypeStruct((2, 2 * half, 2 * LAGS), BF16),
            counts,
            counts,
        ),
        in_specs=[pl.BlockSpec(memory_space=pltpu.SMEM)] + [anywhere] * 2 + [vmem] * 5 + [anywhere],
        out_specs=(vmem, vmem, vmem, vmem),
        scratch_shapes=[
            pltpu.VMEM((2, *raw.shape), F32),
            pltpu.SemaphoreType.DMA((2, chans // 8)),
            pltpu.SemaphoreType.DMA,
        ],
        compiler_params=pltpu.CompilerParams(vmem_limit_bytes=12 * 1024 * 1024),
        name="own",
    )(place, raw, other, *sums, windows, all_tables)


def edge_body(first, place, a_rows, far0, far1, table, sum0, near0, sum1, near1, own_n, far_n, *refs):
    if first:
        keep_ref, other_ref, far_ref, b_rows, g_high, g_low, far_buf, sem = refs
    else:
        keep1, other1, keep_ref, other_ref, far_ref, b_rows, g_high, g_low, far_buf, sem = refs
    chans, _, _, half = far0.shape
    hrows = chans // 2
    b0 = pl.multiple_of(place[0], hrows)
    a_keep = place[1]
    b_rows_at = pl.ds(b0, hrows)
    fetches = [
        pltpu.make_async_copy(source.at[b_rows_at], far_buf.at[k], sem.at[k])
        for k, source in enumerate((far0, far1))
    ]
    for fetch in fetches:
        fetch.start()
    mean = means((sum0, near0, sum1, near1))
    for fetch in fetches:
        fetch.wait()

    def channel(b, carry):
        re, im = whiten(far_buf[0, b], far_buf[1, b], mean, far_n[pl.ds(b0 + b, 1), :])
        for lane, (v, u) in enumerate(zip(re, im)):
            for plane, value in enumerate((v + u, u - v, v)):
                at = pl.ds(plane * WINDOWS * hrows + b, WINDOWS, stride=hrows)
                b_rows[lane, at, :] = value
        return carry

    lax.fori_loop(0, hrows, channel, 0, unroll=True)

    def products(t, carry):
        a0 = t * A_TILE
        for c in range(2 * half // LANE):
            sums = [[None] * 3 for _ in range(A_TILE)]
            for w in range(WINDOWS):
                far = [
                    b_rows[c, pl.ds((k * WINDOWS + w) * hrows, hrows), :] for k in range(3)
                ]
                for j in range(A_TILE):
                    for k in range(3):
                        own = a_rows[c, pl.ds((a0 + j) * (3 * WINDOWS) + k * WINDOWS + w, 1), :]
                        term = own * far[k]
                        sums[j][k] = term if w == 0 else sums[j][k] + term
            for j in range(A_TILE):
                s_im, s_re, s_both = sums[j]
                rows = pl.ds(pl.multiple_of((a0 + j) * hrows, hrows), hrows)
                for part, value in enumerate((s_both + s_re, s_both - s_im)):
                    high = value.astype(BF16)
                    at = slice(part * 2 * half + c * LANE, part * 2 * half + (c + 1) * LANE)
                    g_high[rows, at] = high
                    g_low[rows, at] = (value - high.astype(F32)).astype(BF16)
        return carry

    lax.fori_loop(0, chans // A_TILE, products, 0)
    far_counts = far_n[pl.ds(b0, hrows), :]
    group = 16

    def lagged(t, carry):
        size = group * hrows
        rows = pl.ds(pl.multiple_of(t * size, size), size)

        def project(part):
            at = slice(2 * part * half, 2 * (part + 1) * half)
            both = jnp.dot(g_high[rows, at], table[part], preferred_element_type=F32)
            low = jnp.dot(g_low[rows, at], table[part, :, :LAGS], preferred_element_type=F32)
            return both[:, :LAGS] + both[:, LAGS:] + low

        real = project(0)
        imag = project(1)
        forward = real - imag
        backward = real + imag
        for j in range(group):
            a = t * group + j
            shared = jnp.minimum(far_counts, own_n[pl.ds(a, 1), :])
            scale = (1.0 / math.sqrt(FBAND)) / shared
            at = slice(j * hrows, (j + 1) * hrows)
            far_ref[:, a, :] = backward[at] * scale
            value = forward[at] * scale
            mine = (a >= a_keep) & (a < a_keep + hrows)

            spot = slice(None) if first else b_rows_at

            @pl.when(mine)
            def _():
                keep_ref[a - a_keep, spot, :] = value

            @pl.when(jnp.logical_not(mine))
            def _():
                other_ref[a - (hrows - a_keep), spot, :] = value

        return carry

    lax.fori_loop(0, chans // group, lagged, 0)
    if not first:
        before = pl.ds(pl.multiple_of(hrows - b0, hrows), hrows)
        keep_ref[:, before, :] = keep1[...]
        other_ref[:, before, :] = other1[...]


def edge(place, a_rows, far, table, sums, counts, before=()):
    chans, _, _, half = far[0].shape
    band = 2 * half
    hrows = chans // 2
    vmem = pl.BlockSpec(memory_space=pltpu.VMEM)
    anywhere = pl.BlockSpec(memory_space=pl.ANY)
    mine = jax.ShapeDtypeStruct((hrows, chans if before else hrows, LAGS), F32)
    return pl.pallas_call(
        functools.partial(edge_body, not before),
        out_shape=(mine, mine, jax.ShapeDtypeStruct((hrows, chans, LAGS), F32)),
        in_specs=[pl.BlockSpec(memory_space=pltpu.SMEM), vmem]
        + [anywhere] * 2 + [vmem] * (7 + len(before)),
        out_specs=(vmem, vmem, vmem),
        scratch_shapes=[
            pltpu.VMEM((band // LANE, 3 * WINDOWS * hrows, LANE), F32),
            pltpu.VMEM((chans * hrows, 2 * band), BF16),
            pltpu.VMEM((chans * hrows, 2 * band), BF16),
            pltpu.VMEM((2, hrows, 2, WINDOWS, half), F32),
            pltpu.SemaphoreType.DMA((2,)),
        ],
        compiler_params=pltpu.CompilerParams(vmem_limit_bytes=20 * 1024 * 1024),
        cost_estimate=pl.CostEstimate(flops=1_000_000, bytes_accessed=10_000, transcendentals=0),
        name="edge",
    )(place, a_rows, *far, table, *sums, *counts, *before)


def on_device(raw_spectra, valid_windows):
    chans, _, _, half = raw_spectra.shape
    hrows = chans // 2
    size = lax.axis_size("chan")
    chan_index = lax.axis_index("chan")
    freq_index = lax.axis_index("freq")
    barrier = lax.optimization_barrier

    def to_partner(block, flip):
        return lax.ppermute(block, ("chan", "freq"), edge_route(size, flip))

    def from_partner(block):
        route = [(high, low) for low, high in edge_route(size, 0)]
        return lax.ppermute(block, ("chan", "freq"), route)

    parity = parity_of(chan_index)
    my_round = owner_round(parity, freq_index)
    partner = chan_index ^ (1 << my_round)

    sums = jnp.sum(raw_spectra, axis=0)
    other = swap_freq(raw_spectra)
    far = {}

    def after_z1(sums):
        held, sums = barrier((raw_spectra, sums))
        far["mine"] = from_partner(held)
        return sums

    def after_core(sums):
        far["own"], far["mine"], sums = barrier((other, far["mine"], sums))
        far["other"] = from_partner(far["own"])
        return sums

    sums = sum_over_chan(
        sums, size, ("z1", "z", "y", "core"), {"z1": after_z1, "core": after_core}
    )
    windows = valid_windows.reshape(-1, LANE)

    def at(b0):
        return jnp.stack([b0, freq_index * hrows, chan_index, partner]).astype(jnp.int32)

    all_tables = np.stack(lag_tables())
    all_tables = jnp.asarray(np.concatenate([all_tables, all_tables[:, :half]], axis=1))
    a_rows, table, *counts = whiten_own(at(0), raw_spectra, far["own"], sums, windows, all_tables)

    def work(b0, before=()):
        return edge(at(b0), a_rows, (far["mine"], far["other"]), table, sums, counts, before)

    keep, other, far1 = work((1 - freq_index) * hrows)
    far1 = to_partner(far1, 1)
    keep, other, far2 = work(freq_index * hrows, (keep, other))
    other = swap_freq(other)
    far1, far2 = barrier((far1, far2))
    far2 = to_partner(far2, 0)

    index = lax.broadcasted_iota(jnp.int32, (ROUNDS, 1, 1, 1), 0)
    own_pair = index // 2 == parity
    same_freq = index % 2 == freq_index
    return jnp.where(
        own_pair, jnp.where(same_freq, keep, other), jnp.where(same_freq, far2, far1)
    )


def solution(mesh):
    return jax.shard_map(
        on_device,
        mesh=mesh,
        in_specs=(P("chan", None, None, "freq"), P()),
        out_specs=P(None, ("chan", "freq"), None, None),
        check_vma=False,
    )
```

```python
import functools
import math

import jax
import jax.numpy as jnp
import ml_dtypes
import numpy as np
from jax import lax
from jax.experimental import pallas as pl
from jax.experimental.pallas import tpu as pltpu
from jax.sharding import PartitionSpec as P

F32 = jnp.float32
BF16 = jnp.bfloat16
FBAND = 512
NFFT = 8192
K0 = 164
LAGS = 128
ROUNDS = 4
WINDOWS = 16
CHANNELS = 4096
A_TILE = 4
LANE = 128


def parity_of(index):
    return (index ^ (index >> 1) ^ (index >> 2) ^ (index >> 3)) & 1


def owner_round(parity, freq):
    return 2 * parity + freq


def edge_route(chan_count, flip):
    route = []
    for chan in range(chan_count):
        for freq in range(2):
            far = chan ^ (1 << owner_round(parity_of(chan), freq))
            route.append((chan * 2 + freq, far * 2 + (freq ^ flip)))
    return route


def from_chan(block, source, chan_count):
    return lax.ppermute(block, "chan", [(source(i), i) for i in range(chan_count)])


def step_y(chan, by):
    return (chan & ~6) | (((chan >> 1) + by) % 4 << 1)


def step_z(chan, by):
    return (chan & ~56) | (((chan >> 3) + by) % 8 << 3)


def sum_over_chan(sums, size, order, hooks):
    top = size // 2
    steps = {
        "core": [lambda i: i ^ 1],
        "z1": [lambda i: i ^ 8],
        "z": [lambda i: step_z(i, 4), lambda i: step_z(i, 2), lambda i: step_z(i, -2)],
        "y": [lambda i: step_y(i, 2), lambda i: step_y(i, 1), lambda i: step_y(i, -1)],
        "y2": [lambda i: i ^ 4],
        "y1": [lambda i: i ^ 2],
    }
    for name in order:
        sums = sum((from_chan(sums, source, size) for source in steps[name]), sums)
        sums = lax.optimization_barrier(sums)
        if name in hooks:
            sums = hooks[name](sums)
    far = swap_freq(sums)
    near = from_chan(sums, lambda i: i ^ top, size)
    diagonal = lax.ppermute(
        sums, ("chan", "freq"), [(d, d ^ (2 * top) ^ 1) for d in range(2 * size)]
    )
    return sums, near, far, diagonal


def swap_freq(block):
    return lax.ppermute(block, "freq", [(0, 1), (1, 0)])


def lag_tables():
    bins = K0 + np.arange(FBAND)
    lags = np.arange(LAGS) - LAGS // 2
    angles = (bins[:, None] * lags[None, :] % NFFT) * (2.0 * math.pi / NFFT)
    tables = []
    for table in (np.cos(angles), np.sin(angles)):
        high = table.astype(ml_dtypes.bfloat16)
        low = (table - high.astype(np.float64)).astype(ml_dtypes.bfloat16)
        tables.append(np.concatenate([high, low], axis=1))
    return tables


def channel_counts(windows, chan, chans):
    per_row = LANE // chans
    row = windows[pl.ds(chan // per_row, 1), :]
    lanes = lax.broadcasted_iota(jnp.int32, (chans, LANE), 1)
    first = lax.broadcasted_iota(jnp.int32, (chans, LANE), 0) + chan % per_row * chans
    picked = jnp.where(lanes == first, row, 0).astype(F32)
    return jnp.sum(picked, axis=1, keepdims=True)


def means(sums):
    sum0, near0, sum1, near1 = sums
    return [
        (total[part] + near[part]) * (1.0 / CHANNELS)
        for total, near in ((sum0, near0), (sum1, near1))
        for part in range(2)
    ]


def whiten(low, high, mean, count):
    re0, im0 = low[0] - mean[0], low[1] - mean[1]
    re1, im1 = high[0] - mean[2], high[1] - mean[3]
    energy = jnp.sum(re0 * re0 + im0 * im0 + re1 * re1 + im1 * im1, axis=1, keepdims=True)
    scale = lax.rsqrt(energy * (1.0 / FBAND) + 1e-06)
    window = lax.broadcasted_iota(jnp.int32, (WINDOWS, LANE), 0).astype(F32)
    scale = jnp.where(window < count, scale, 0.0)
    re, im = [], []
    for real, imag in ((re0, im0), (re1, im1)):
        for lane in range(0, real.shape[1], LANE):
            re.append(real[:, lane : lane + LANE] * scale)
            im.append(imag[:, lane : lane + LANE] * scale)
    return re, im


def own_body(
    place, raw, other, sum0, near0, sum1, near1, windows, all_tables,
    a_rows, table, own_n, far_n, buf, sem, table_sem,
):
    chans, _, _, half = raw.shape
    step = 8
    fetches = []
    for c in range(chans // step):
        at = pl.ds(c * step, step)
        for k, source in enumerate((raw, other)):
            fetches.append(pltpu.make_async_copy(source.at[at], buf.at[k, at], sem.at[k, c]))
    for fetch in fetches:
        fetch.start()
    first_bin = pl.multiple_of(place[1] * (half // (chans // 2)), half)
    table_fetch = pltpu.make_async_copy(
        all_tables.at[:, pl.ds(first_bin, 2 * half), :], table, table_sem
    )
    table_fetch.start()
    own_n[...] = jnp.broadcast_to(channel_counts(windows, place[2], chans), (chans, LANE))
    far_n[...] = jnp.broadcast_to(channel_counts(windows, place[3], chans), (chans, LANE))
    mean = means((sum0, near0, sum1, near1))
    for c in range(chans // step):
        fetches[2 * c].wait()
        fetches[2 * c + 1].wait()

        def channel(k, carry):
            a = c * step + k
            re, im = whiten(buf[0, a], buf[1, a], mean, own_n[pl.ds(a, 1), :])
            for lane, (v, u) in enumerate(zip(re, im)):
                for plane, value in enumerate((v, u, v + u)):
                    first = pl.multiple_of(a * (3 * WINDOWS) + plane * WINDOWS, WINDOWS)
                    a_rows[lane, pl.ds(first, WINDOWS), :] = value
            return carry

        lax.fori_loop(0, step, channel, 0, unroll=True)
    table_fetch.wait()


def whiten_own(place, raw, other, sums, windows, all_tables):
    chans, _, _, half = raw.shape
    vmem = pl.BlockSpec(memory_space=pltpu.VMEM)
    anywhere = pl.BlockSpec(memory_space=pl.ANY)
    counts = jax.ShapeDtypeStruct((chans, LANE), F32)
    return pl.pallas_call(
        own_body,
        out_shape=(
            jax.ShapeDtypeStruct((2 * half // LANE, chans * 3 * WINDOWS, LANE), F32),
            jax.ShapeDtypeStruct((2, 2 * half, 2 * LAGS), BF16),
            counts,
            counts,
        ),
        in_specs=[pl.BlockSpec(memory_space=pltpu.SMEM)] + [anywhere] * 2 + [vmem] * 5 + [anywhere],
        out_specs=(vmem, vmem, vmem, vmem),
        scratch_shapes=[
            pltpu.VMEM((2, *raw.shape), F32),
            pltpu.SemaphoreType.DMA((2, chans // 8)),
            pltpu.SemaphoreType.DMA,
        ],
        compiler_params=pltpu.CompilerParams(vmem_limit_bytes=12 * 1024 * 1024),
        name="own",
    )(place, raw, other, *sums, windows, all_tables)


def edge_body(first, place, a_rows, far0, far1, table, sum0, near0, sum1, near1, own_n, far_n, *refs):
    if first:
        keep_ref, other_ref, far_ref, b_rows, g_high, g_low, far_buf, sem = refs
    else:
        keep1, other1, keep_ref, other_ref, far_ref, b_rows, g_high, g_low, far_buf, sem = refs
    chans, _, _, half = far0.shape
    hrows = chans // 2
    b0 = pl.multiple_of(place[0], hrows)
    a_keep = place[1]
    b_rows_at = pl.ds(b0, hrows)
    fetches = [
        pltpu.make_async_copy(source.at[b_rows_at], far_buf.at[k], sem.at[k])
        for k, source in enumerate((far0, far1))
    ]
    for fetch in fetches:
        fetch.start()
    mean = means((sum0, near0, sum1, near1))
    for fetch in fetches:
        fetch.wait()

    def channel(b, carry):
        re, im = whiten(far_buf[0, b], far_buf[1, b], mean, far_n[pl.ds(b0 + b, 1), :])
        for lane, (v, u) in enumerate(zip(re, im)):
            for plane, value in enumerate((v + u, u - v, v)):
                at = pl.ds(plane * WINDOWS * hrows + b, WINDOWS, stride=hrows)
                b_rows[lane, at, :] = value
        return carry

    lax.fori_loop(0, hrows, channel, 0, unroll=True)

    def products(t, carry):
        a0 = t * A_TILE
        for c in range(2 * half // LANE):
            sums = [[None] * 3 for _ in range(A_TILE)]
            for w in range(WINDOWS):
                far = [
                    b_rows[c, pl.ds((k * WINDOWS + w) * hrows, hrows), :] for k in range(3)
                ]
                for j in range(A_TILE):
                    for k in range(3):
                        own = a_rows[c, pl.ds((a0 + j) * (3 * WINDOWS) + k * WINDOWS + w, 1), :]
                        term = own * far[k]
                        sums[j][k] = term if w == 0 else sums[j][k] + term
            for j in range(A_TILE):
                s_im, s_re, s_both = sums[j]
                rows = pl.ds(pl.multiple_of((a0 + j) * hrows, hrows), hrows)
                for part, value in enumerate((s_both + s_re, s_both - s_im)):
                    high = value.astype(BF16)
                    at = slice(part * 2 * half + c * LANE, part * 2 * half + (c + 1) * LANE)
                    g_high[rows, at] = high
                    g_low[rows, at] = (value - high.astype(F32)).astype(BF16)
        return carry

    lax.fori_loop(0, chans // A_TILE, products, 0)
    far_counts = far_n[pl.ds(b0, hrows), :]
    group = 32

    def lagged(t, carry):
        size = group * hrows
        rows = pl.ds(pl.multiple_of(t * size, size), size)

        def project(part):
            at = slice(2 * part * half, 2 * (part + 1) * half)
            both = jnp.dot(g_high[rows, at], table[part], preferred_element_type=F32)
            low = jnp.dot(g_low[rows, at], table[part, :, :LAGS], preferred_element_type=F32)
            return both[:, :LAGS] + both[:, LAGS:] + low

        real = project(0)
        imag = project(1)
        forward = real - imag
        backward = real + imag
        for j in range(group):
            a = t * group + j
            shared = jnp.minimum(far_counts, own_n[pl.ds(a, 1), :])
            scale = (1.0 / math.sqrt(FBAND)) / shared
            at = slice(j * hrows, (j + 1) * hrows)
            far_ref[:, a, :] = backward[at] * scale
            value = forward[at] * scale
            mine = (a >= a_keep) & (a < a_keep + hrows)

            spot = slice(None) if first else b_rows_at

            @pl.when(mine)
            def _():
                keep_ref[a - a_keep, spot, :] = value

            @pl.when(jnp.logical_not(mine))
            def _():
                other_ref[a - (hrows - a_keep), spot, :] = value

        return carry

    lax.fori_loop(0, chans // group, lagged, 0)
    if not first:
        before = pl.ds(pl.multiple_of(hrows - b0, hrows), hrows)
        keep_ref[:, before, :] = keep1[...]
        other_ref[:, before, :] = other1[...]


def edge(place, a_rows, far, table, sums, counts, before=()):
    chans, _, _, half = far[0].shape
    band = 2 * half
    hrows = chans // 2
    vmem = pl.BlockSpec(memory_space=pltpu.VMEM)
    anywhere = pl.BlockSpec(memory_space=pl.ANY)
    mine = jax.ShapeDtypeStruct((hrows, chans if before else hrows, LAGS), F32)
    return pl.pallas_call(
        functools.partial(edge_body, not before),
        out_shape=(mine, mine, jax.ShapeDtypeStruct((hrows, chans, LAGS), F32)),
        in_specs=[pl.BlockSpec(memory_space=pltpu.SMEM), vmem]
        + [anywhere] * 2 + [vmem] * (7 + len(before)),
        out_specs=(vmem, vmem, vmem),
        scratch_shapes=[
            pltpu.VMEM((band // LANE, 3 * WINDOWS * hrows, LANE), F32),
            pltpu.VMEM((chans * hrows, 2 * band), BF16),
            pltpu.VMEM((chans * hrows, 2 * band), BF16),
            pltpu.VMEM((2, hrows, 2, WINDOWS, half), F32),
            pltpu.SemaphoreType.DMA((2,)),
        ],
        compiler_params=pltpu.CompilerParams(vmem_limit_bytes=20 * 1024 * 1024),
        cost_estimate=pl.CostEstimate(flops=1_000_000, bytes_accessed=10_000, transcendentals=0),
        name="edge",
    )(place, a_rows, *far, table, *sums, *counts, *before)


def on_device(raw_spectra, valid_windows):
    chans, _, _, half = raw_spectra.shape
    hrows = chans // 2
    size = lax.axis_size("chan")
    chan_index = lax.axis_index("chan")
    freq_index = lax.axis_index("freq")
    barrier = lax.optimization_barrier

    def to_partner(block, flip):
        return lax.ppermute(block, ("chan", "freq"), edge_route(size, flip))

    def from_partner(block):
        route = [(high, low) for low, high in edge_route(size, 0)]
        return lax.ppermute(block, ("chan", "freq"), route)

    parity = parity_of(chan_index)
    my_round = owner_round(parity, freq_index)
    partner = chan_index ^ (1 << my_round)

    sums = jnp.sum(raw_spectra, axis=0)
    other = swap_freq(raw_spectra)
    far = {}

    def after_z1(sums):
        held, sums = barrier((raw_spectra, sums))
        far["mine"] = from_partner(held)
        return sums

    def after_core(sums):
        far["own"], far["mine"], sums = barrier((other, far["mine"], sums))
        far["other"] = from_partner(far["own"])
        return sums

    sums = sum_over_chan(
        sums, size, ("z1", "z", "y", "core"), {"z1": after_z1, "core": after_core}
    )
    windows = valid_windows.reshape(-1, LANE)

    def at(b0):
        return jnp.stack([b0, freq_index * hrows, chan_index, partner]).astype(jnp.int32)

    all_tables = np.stack(lag_tables())
    all_tables = jnp.asarray(np.concatenate([all_tables, all_tables[:, :half]], axis=1))
    a_rows, table, *counts = whiten_own(at(0), raw_spectra, far["own"], sums, windows, all_tables)

    def work(b0, before=()):
        return edge(at(b0), a_rows, (far["mine"], far["other"]), table, sums, counts, before)

    keep, other, far1 = work((1 - freq_index) * hrows)
    far1 = to_partner(far1, 1)
    keep, other, far2 = work(freq_index * hrows, (keep, other))
    other = swap_freq(other)
    far1, far2 = barrier((far1, far2))
    far2 = to_partner(far2, 0)

    index = lax.broadcasted_iota(jnp.int32, (ROUNDS, 1, 1, 1), 0)
    own_pair = index // 2 == parity
    same_freq = index % 2 == freq_index
    return jnp.where(
        own_pair, jnp.where(same_freq, keep, other), jnp.where(same_freq, far2, far1)
    )


def solution(mesh):
    return jax.shard_map(
        on_device,
        mesh=mesh,
        in_specs=(P("chan", None, None, "freq"), P()),
        out_specs=P(None, ("chan", "freq"), None, None),
        check_vma=False,
    )
```

```python
import functools
import math

import jax
import jax.numpy as jnp
import ml_dtypes
import numpy as np
from jax import lax
from jax.experimental import pallas as pl
from jax.experimental.pallas import tpu as pltpu
from jax.sharding import PartitionSpec as P

F32 = jnp.float32
BF16 = jnp.bfloat16
FBAND = 512
NFFT = 8192
K0 = 164
LAGS = 128
ROUNDS = 4
WINDOWS = 16
CHANNELS = 4096
A_TILE = 4
LANE = 128


def parity_of(index):
    return (index ^ (index >> 1) ^ (index >> 2) ^ (index >> 3)) & 1


def owner_round(parity, freq):
    return 2 * parity + freq


def edge_route(chan_count, flip):
    route = []
    for chan in range(chan_count):
        for freq in range(2):
            far = chan ^ (1 << owner_round(parity_of(chan), freq))
            route.append((chan * 2 + freq, far * 2 + (freq ^ flip)))
    return route


def from_chan(block, source, chan_count):
    return lax.ppermute(block, "chan", [(source(i), i) for i in range(chan_count)])


def step_y(chan, by):
    return (chan & ~6) | (((chan >> 1) + by) % 4 << 1)


def step_z(chan, by):
    return (chan & ~56) | (((chan >> 3) + by) % 8 << 3)


def sum_over_chan(sums, size, order, hooks):
    top = size // 2
    steps = {
        "core": [lambda i: i ^ 1],
        "z1": [lambda i: i ^ 8],
        "z": [lambda i: step_z(i, 4), lambda i: step_z(i, 2), lambda i: step_z(i, -2)],
        "y": [lambda i: step_y(i, 2), lambda i: step_y(i, 1), lambda i: step_y(i, -1)],
        "y2": [lambda i: i ^ 4],
        "y1": [lambda i: i ^ 2],
    }
    for name in order:
        sums = sum((from_chan(sums, source, size) for source in steps[name]), sums)
        sums = lax.optimization_barrier(sums)
        if name in hooks:
            sums = hooks[name](sums)
    far = swap_freq(sums)
    near = from_chan(sums, lambda i: i ^ top, size)
    diagonal = lax.ppermute(
        sums, ("chan", "freq"), [(d, d ^ (2 * top) ^ 1) for d in range(2 * size)]
    )
    return sums, near, far, diagonal


def swap_freq(block):
    return lax.ppermute(block, "freq", [(0, 1), (1, 0)])


def lag_tables():
    bins = K0 + np.arange(FBAND)
    lags = np.arange(LAGS) - LAGS // 2
    angles = (bins[:, None] * lags[None, :] % NFFT) * (2.0 * math.pi / NFFT)
    tables = []
    for table in (np.cos(angles), np.sin(angles)):
        high = table.astype(ml_dtypes.bfloat16)
        low = (table - high.astype(np.float64)).astype(ml_dtypes.bfloat16)
        tables.append(np.concatenate([high, low], axis=1))
    return tables


def channel_counts(windows, chan, chans):
    per_row = LANE // chans
    row = windows[pl.ds(chan // per_row, 1), :]
    lanes = lax.broadcasted_iota(jnp.int32, (chans, LANE), 1)
    first = lax.broadcasted_iota(jnp.int32, (chans, LANE), 0) + chan % per_row * chans
    picked = jnp.where(lanes == first, row, 0).astype(F32)
    return jnp.sum(picked, axis=1, keepdims=True)


def means(sums):
    sum0, near0, sum1, near1 = sums
    return [
        (total[part] + near[part]) * (1.0 / CHANNELS)
        for total, near in ((sum0, near0), (sum1, near1))
        for part in range(2)
    ]


def whiten(low, high, mean, count):
    re0, im0 = low[0] - mean[0], low[1] - mean[1]
    re1, im1 = high[0] - mean[2], high[1] - mean[3]
    energy = jnp.sum(re0 * re0 + im0 * im0 + re1 * re1 + im1 * im1, axis=1, keepdims=True)
    scale = lax.rsqrt(energy * (1.0 / FBAND) + 1e-06)
    window = lax.broadcasted_iota(jnp.int32, (WINDOWS, LANE), 0).astype(F32)
    scale = jnp.where(window < count, scale, 0.0)
    re, im = [], []
    for real, imag in ((re0, im0), (re1, im1)):
        for lane in range(0, real.shape[1], LANE):
            re.append(real[:, lane : lane + LANE] * scale)
            im.append(imag[:, lane : lane + LANE] * scale)
    return re, im


def own_body(
    place, raw, other, sum0, near0, sum1, near1, windows, all_tables,
    a_rows, table, own_n, far_n, buf, sem, table_sem,
):
    chans, _, _, half = raw.shape
    hrows = chans // 2
    step = 8
    fetches = []
    for c in range(chans // step):
        at = pl.ds(c * step, step)
        for k, source in enumerate((raw, other)):
            fetches.append(pltpu.make_async_copy(source.at[at], buf.at[k, at], sem.at[k, c]))
    for fetch in fetches:
        fetch.start()
    first_bin = pl.multiple_of(place[1] * (half // hrows), half)
    table_fetches = [
        pltpu.make_async_copy(
            all_tables.at[:, pl.ds(bin_at, half), :],
            table.at[:, k * half : (k + 1) * half, :],
            table_sem.at[k],
        )
        for k, bin_at in enumerate((first_bin, pl.multiple_of(half - first_bin, half)))
    ]
    for fetch in table_fetches:
        fetch.start()
    own_n[...] = jnp.broadcast_to(channel_counts(windows, place[2], chans), (chans, LANE))
    far_n[...] = jnp.broadcast_to(channel_counts(windows, place[3], chans), (chans, LANE))
    mean = means((sum0, near0, sum1, near1))
    for c in range(chans // step):
        fetches[2 * c].wait()
        fetches[2 * c + 1].wait()

        def channel(k, carry):
            a = c * step + k
            re, im = whiten(buf[0, a], buf[1, a], mean, own_n[pl.ds(a, 1), :])
            for lane, (v, u) in enumerate(zip(re, im)):
                for plane, value in enumerate((v, u, v + u)):
                    first = pl.multiple_of(a * (3 * WINDOWS) + plane * WINDOWS, WINDOWS)
                    a_rows[lane, pl.ds(first, WINDOWS), :] = value
            return carry

        lax.fori_loop(0, step, channel, 0, unroll=True)
    for fetch in table_fetches:
        fetch.wait()


def whiten_own(place, raw, other, sums, windows, all_tables):
    chans, _, _, half = raw.shape
    vmem = pl.BlockSpec(memory_space=pltpu.VMEM)
    anywhere = pl.BlockSpec(memory_space=pl.ANY)
    counts = jax.ShapeDtypeStruct((chans, LANE), F32)
    return pl.pallas_call(
        own_body,
        out_shape=(
            jax.ShapeDtypeStruct((2 * half // LANE, chans * 3 * WINDOWS, LANE), F32),
            jax.ShapeDtypeStruct((2, 2 * half, 2 * LAGS), BF16),
            counts,
            counts,
        ),
        in_specs=[pl.BlockSpec(memory_space=pltpu.SMEM)] + [anywhere] * 2 + [vmem] * 5 + [anywhere],
        out_specs=(vmem, vmem, vmem, vmem),
        scratch_shapes=[
            pltpu.VMEM((2, *raw.shape), F32),
            pltpu.SemaphoreType.DMA((2, chans // 8)),
            pltpu.SemaphoreType.DMA((2,)),
        ],
        compiler_params=pltpu.CompilerParams(vmem_limit_bytes=12 * 1024 * 1024),
        name="own",
    )(place, raw, other, *sums, windows, all_tables)


def edge_body(first, place, a_rows, far0, far1, table, sum0, near0, sum1, near1, own_n, far_n, *refs):
    if first:
        keep_ref, other_ref, far_ref, b_rows, g_high, g_low, far_buf, sem = refs
    else:
        keep1, other1, keep_ref, other_ref, far_ref, b_rows, g_high, g_low, far_buf, sem = refs
    chans, _, _, half = far0.shape
    hrows = chans // 2
    b0 = pl.multiple_of(place[0], hrows)
    a_keep = place[1]
    b_rows_at = pl.ds(b0, hrows)
    fetches = [
        pltpu.make_async_copy(source.at[b_rows_at], far_buf.at[k], sem.at[k])
        for k, source in enumerate((far0, far1))
    ]
    for fetch in fetches:
        fetch.start()
    mean = means((sum0, near0, sum1, near1))
    for fetch in fetches:
        fetch.wait()

    def channel(b, carry):
        re, im = whiten(far_buf[0, b], far_buf[1, b], mean, far_n[pl.ds(b0 + b, 1), :])
        for lane, (v, u) in enumerate(zip(re, im)):
            for plane, value in enumerate((v + u, u - v, v)):
                at = pl.ds(plane * WINDOWS * hrows + b, WINDOWS, stride=hrows)
                b_rows[lane, at, :] = value
        return carry

    lax.fori_loop(0, hrows, channel, 0, unroll=True)

    def products(t, carry):
        a0 = t * A_TILE
        for c in range(2 * half // LANE):
            sums = [[None] * 3 for _ in range(A_TILE)]
            for w in range(WINDOWS):
                far = [
                    b_rows[c, pl.ds((k * WINDOWS + w) * hrows, hrows), :] for k in range(3)
                ]
                for j in range(A_TILE):
                    for k in range(3):
                        own = a_rows[c, pl.ds((a0 + j) * (3 * WINDOWS) + k * WINDOWS + w, 1), :]
                        term = own * far[k]
                        sums[j][k] = term if w == 0 else sums[j][k] + term
            for j in range(A_TILE):
                s_im, s_re, s_both = sums[j]
                rows = pl.ds(pl.multiple_of((a0 + j) * hrows, hrows), hrows)
                for part, value in enumerate((s_both + s_re, s_both - s_im)):
                    high = value.astype(BF16)
                    at = slice(part * 2 * half + c * LANE, part * 2 * half + (c + 1) * LANE)
                    g_high[rows, at] = high
                    g_low[rows, at] = (value - high.astype(F32)).astype(BF16)
        return carry

    lax.fori_loop(0, chans // A_TILE, products, 0)
    far_counts = far_n[pl.ds(b0, hrows), :]
    group = 32

    def lagged(t, carry):
        size = group * hrows
        rows = pl.ds(pl.multiple_of(t * size, size), size)

        def project(part):
            at = slice(2 * part * half, 2 * (part + 1) * half)
            both = jnp.dot(g_high[rows, at], table[part], preferred_element_type=F32)
            low = jnp.dot(g_low[rows, at], table[part, :, :LAGS], preferred_element_type=F32)
            return both[:, :LAGS] + both[:, LAGS:] + low

        real = project(0)
        imag = project(1)
        forward = real - imag
        backward = real + imag
        for j in range(group):
            a = t * group + j
            shared = jnp.minimum(far_counts, own_n[pl.ds(a, 1), :])
            scale = (1.0 / math.sqrt(FBAND)) / shared
            at = slice(j * hrows, (j + 1) * hrows)
            far_ref[:, a, :] = backward[at] * scale
            value = forward[at] * scale
            mine = (a >= a_keep) & (a < a_keep + hrows)

            spot = slice(None) if first else b_rows_at

            @pl.when(mine)
            def _():
                keep_ref[a - a_keep, spot, :] = value

            @pl.when(jnp.logical_not(mine))
            def _():
                other_ref[a - (hrows - a_keep), spot, :] = value

        return carry

    lax.fori_loop(0, chans // group, lagged, 0)
    if not first:
        before = pl.ds(pl.multiple_of(hrows - b0, hrows), hrows)
        keep_ref[:, before, :] = keep1[...]
        other_ref[:, before, :] = other1[...]


def edge(place, a_rows, far, table, sums, counts, before=()):
    chans, _, _, half = far[0].shape
    band = 2 * half
    hrows = chans // 2
    vmem = pl.BlockSpec(memory_space=pltpu.VMEM)
    anywhere = pl.BlockSpec(memory_space=pl.ANY)
    mine = jax.ShapeDtypeStruct((hrows, chans if before else hrows, LAGS), F32)
    return pl.pallas_call(
        functools.partial(edge_body, not before),
        out_shape=(mine, mine, jax.ShapeDtypeStruct((hrows, chans, LAGS), F32)),
        in_specs=[pl.BlockSpec(memory_space=pltpu.SMEM), vmem]
        + [anywhere] * 2 + [vmem] * (7 + len(before)),
        out_specs=(vmem, vmem, vmem),
        scratch_shapes=[
            pltpu.VMEM((band // LANE, 3 * WINDOWS * hrows, LANE), F32),
            pltpu.VMEM((chans * hrows, 2 * band), BF16),
            pltpu.VMEM((chans * hrows, 2 * band), BF16),
            pltpu.VMEM((2, hrows, 2, WINDOWS, half), F32),
            pltpu.SemaphoreType.DMA((2,)),
        ],
        compiler_params=pltpu.CompilerParams(vmem_limit_bytes=20 * 1024 * 1024),
        cost_estimate=pl.CostEstimate(flops=1_000_000, bytes_accessed=10_000, transcendentals=0),
        name="edge",
    )(place, a_rows, *far, table, *sums, *counts, *before)


def on_device(raw_spectra, valid_windows):
    chans, _, _, half = raw_spectra.shape
    hrows = chans // 2
    size = lax.axis_size("chan")
    chan_index = lax.axis_index("chan")
    freq_index = lax.axis_index("freq")
    barrier = lax.optimization_barrier

    def to_partner(block, flip):
        return lax.ppermute(block, ("chan", "freq"), edge_route(size, flip))

    def from_partner(block):
        route = [(high, low) for low, high in edge_route(size, 0)]
        return lax.ppermute(block, ("chan", "freq"), route)

    parity = parity_of(chan_index)
    my_round = owner_round(parity, freq_index)
    partner = chan_index ^ (1 << my_round)

    sums = jnp.sum(raw_spectra, axis=0)
    other = swap_freq(raw_spectra)
    far = {}

    def after_z1(sums):
        held, sums = barrier((raw_spectra, sums))
        far["mine"] = from_partner(held)
        return sums

    def after_core(sums):
        far["own"], far["mine"], sums = barrier((other, far["mine"], sums))
        far["other"] = from_partner(far["own"])
        return sums

    sums = sum_over_chan(
        sums, size, ("z1", "z", "y", "core"), {"z1": after_z1, "core": after_core}
    )
    windows = valid_windows.reshape(-1, LANE)

    def at(b0):
        return jnp.stack([b0, freq_index * hrows, chan_index, partner]).astype(jnp.int32)

    all_tables = jnp.asarray(np.stack(lag_tables()))
    a_rows, table, *counts = whiten_own(at(0), raw_spectra, far["own"], sums, windows, all_tables)

    def work(b0, before=()):
        return edge(at(b0), a_rows, (far["mine"], far["other"]), table, sums, counts, before)

    keep, other, far1 = work((1 - freq_index) * hrows)
    far1 = to_partner(far1, 1)
    keep, other, far2 = work(freq_index * hrows, (keep, other))
    other = swap_freq(other)
    far1, far2 = barrier((far1, far2))
    far2 = to_partner(far2, 0)

    index = lax.broadcasted_iota(jnp.int32, (ROUNDS, 1, 1, 1), 0)
    own_pair = index // 2 == parity
    same_freq = index % 2 == freq_index
    return jnp.where(
        own_pair, jnp.where(same_freq, keep, other), jnp.where(same_freq, far2, far1)
    )


def solution(mesh):
    return jax.shard_map(
        on_device,
        mesh=mesh,
        in_specs=(P("chan", None, None, "freq"), P()),
        out_specs=P(None, ("chan", "freq"), None, None),
        check_vma=False,
    )
```
